512 devices in a mesh: row: 16 (over z, x_hi), col: 32 (over y, x_lo, core).
Axes of the slice: x: 4 (x_hi: 2, x_lo: 2; x = x_hi * 2 + x_lo), y: 8, z: 8, core: 2. Of those that a mesh axis runs over, the one named last changes fastest.
Arguments:
- matrix: float32 [16384, 16384], P('row', 'col'), as said below
- moves: int32 [1, 64], replicated, may hold values from 0 to 63, as said below
Outputs:
- result: float32 [16384, 16384], P('row', 'col')
The draws below stay inside these ranges and needn't reach their ends.
Inputs may be any that keep to these rules, and one draw needn't show every extreme that they name: matrix is symmetric. Each moves[t] is a permutation of the 64 slots made of two rounds of swaps: first of some pairs of slots (2k+1, 2k+2), then of some pairs (2k, 2k+1).
All inputs are finite; a program needn't handle non-finite values.
Results may differ from the reference program's by a relative error of at most 0.0001.
Values sent between devices are 32-bit elements; how exact they have to be, the bound alone decides.
No kernel may reach another device: no remote copies, remote signals or barrier semaphores. Data moves between devices by JAX's collectives and lax.ppermute only.
A program may use at most 64 MiB of HBM per device.

```python
import math
import jax
import jax.numpy as jnp
from jax import lax

BLOCK = 256
NEWTON = 3
STEPS = 1
BLOCKS = 64
ORDER = 16384


def draw_matrix(key, part):
    key = jax.random.fold_in(key, 11)
    raw = jax.random.normal(key, (ORDER, ORDER), jnp.float32)
    return (raw + raw.T) * 0.7071


def draw_moves(key, part):
    key = jax.random.fold_in(key, 23)
    first_key, second_key = jax.random.split(key)
    cross = jax.random.randint(first_key, (STEPS, BLOCKS // 2), 0, 2)
    inner = jax.random.randint(second_key, (STEPS, BLOCKS // 2), 0, 2)
    slots = jnp.arange(BLOCKS, dtype=jnp.int32)
    oddness = slots % 2
    pair_one = jnp.where(oddness == 1, (slots - 1) // 2, (slots - 2) // 2)
    usable = jnp.where(oddness == 1, slots + 1 < BLOCKS, slots > 0).astype(jnp.int32)
    flags = jnp.take(cross, jnp.clip(pair_one, 0, BLOCKS // 2 - 1), axis=1) * usable[None, :]
    middle = jnp.where(flags == 1, jnp.where(oddness == 1, slots + 1, slots - 1)[None, :], slots[None, :])
    second_flags = jnp.take_along_axis(inner, middle // 2, axis=1)
    final = jnp.where(second_flags == 1, middle + 1 - 2 * (middle % 2), middle)
    return final.astype(jnp.int32)


def setup_inputs(seed: int = 0) -> dict:
    key_of = jax.random.split(jax.random.key(seed), 3)
    matrix = draw_matrix(jax.random.fold_in(key_of[2], 71), 0)
    moves = draw_moves(jax.random.fold_in(key_of[2], 71), 0)
    return dict(matrix=matrix, moves=moves)


def newton_step(root, gram):
    highest = lax.Precision.HIGHEST
    inner = jnp.dot(gram, root, precision=highest)
    inner = jnp.dot(root, inner, precision=highest)
    inner = jnp.dot(root, inner, precision=highest)
    return 1.5 * root - 0.5 * inner

def make_factors(upper):
    highest = lax.Precision.HIGHEST
    width = upper.shape[0]
    identity = jnp.eye(width, dtype=jnp.float32)
    coupling = upper * lax.rsqrt(jnp.sum(upper * upper) / width + 1e-06)
    left_gram = identity + jnp.dot(coupling, coupling.T, precision=highest)
    right_gram = identity + jnp.dot(coupling.T, coupling, precision=highest)
    left_root = identity * (1.0 / math.sqrt(5.0))
    right_root = left_root
    for sweep in range(NEWTON):
        left_root = newton_step(left_root, left_gram)
        right_root = newton_step(right_root, right_gram)
    return (left_root, right_root, coupling)

def assemble(left_root, right_root, coupling):
    highest = lax.Precision.HIGHEST
    top = jnp.concatenate([left_root, -jnp.dot(coupling, right_root, precision=highest)], axis=1)
    bottom = jnp.concatenate([jnp.dot(coupling.T, left_root, precision=highest), right_root], axis=1)
    return jnp.concatenate([top, bottom], axis=0)

def make_rotation(upper):
    left_root, right_root, coupling = make_factors(upper)
    return assemble(left_root, right_root, coupling)

def source_slots(order):
    count = order.shape[0]
    slots = jnp.arange(count, dtype=jnp.int32)
    hits = order[None, :] == slots[:, None]
    return lax.optimization_barrier(jnp.sum(jnp.where(hits, slots[None, :], 0), axis=1)).astype(jnp.int32)

def reference(matrix, moves):
    highest = lax.Precision.HIGHEST
    pair_count = BLOCKS // 2
    span = 2 * BLOCK
    current = matrix
    for sweep in range(STEPS):
        grouped = current.reshape(pair_count, span, pair_count, span)
        indices = jnp.arange(pair_count)
        pivots = grouped[indices, :, indices, :]
        uppers = pivots[:, :BLOCK, BLOCK:]
        rotations = jax.vmap(make_rotation)(uppers)
        turned = jnp.einsum('kji,kjc->kic', rotations, current.reshape(pair_count, span, ORDER), precision=highest)
        turned = turned.reshape(ORDER, pair_count, span)
        current = jnp.einsum('rkj,kji->rki', turned, rotations, precision=highest).reshape(ORDER, ORDER)
        sources = source_slots(moves[sweep])
        pieces = current.reshape(BLOCKS, BLOCK, BLOCKS, BLOCK)
        pieces = jnp.take(jnp.take(pieces, sources, axis=0), sources, axis=2)
        current = pieces.reshape(ORDER, ORDER)
    return current
```

```python
import functools
import math

import jax
import jax.numpy as jnp
from jax import lax
from jax.experimental import pallas as pl
from jax.experimental.pallas import tpu as pltpu
from jax.sharding import PartitionSpec as P

BLOCK = 256
SPAN = 2 * BLOCK
AXES = ("row", "col")
VMEM_LIMIT = 32 * 1024 * 1024


def split(x):
    high = x.astype(jnp.bfloat16)
    low = (x - high.astype(jnp.float32)).astype(jnp.bfloat16)
    return high, low


def mul(a, b):
    dot = functools.partial(jnp.dot, preferred_element_type=jnp.float32)
    return dot(a[0], b[0]) + (dot(a[0], b[1]) + dot(a[1], b[0]))


def identity():
    rows = lax.broadcasted_iota(jnp.int32, (BLOCK, BLOCK), 0)
    columns = lax.broadcasted_iota(jnp.int32, (BLOCK, BLOCK), 1)
    return jnp.where(rows == columns, 1.0, 0.0).astype(jnp.float32)


def factors(uppers):
    eye = identity()
    first = 1.0 / math.sqrt(5.0)
    alpha, beta = 1.5 * first, -0.5 * first**3
    couplings, grams = [], []
    for upper in uppers:
        total = jnp.sum(jnp.sum(upper * upper, axis=1, keepdims=True), axis=0, keepdims=True)
        coupling = upper * lax.rsqrt(total / BLOCK + 1e-06)
        here, turned = split(coupling), split(coupling.T)
        couplings.append(here)
        grams.append(eye + mul(here, turned))
        grams.append(eye + mul(turned, here))
    parts = [split(gram) for gram in grams]
    squares = [mul(part, part) for part in parts]
    square_parts = [split(square) for square in squares]
    inner = [
        split(1.5 * alpha * beta**2 * gram + 0.5 * beta**3 * square) for gram, square in zip(grams, squares)
    ]
    seconds = [
        1.5 * alpha * eye + (1.5 * beta - 0.5 * alpha**3) * gram - 1.5 * alpha**2 * beta * square - mul(part, rest)
        for gram, square, part, rest in zip(grams, squares, square_parts, inner)
    ]
    second_parts = [split(second) for second in seconds]
    twice = [split(mul(part, part)) for part in second_parts]
    scaled = [split(mul(gram, part)) for gram, part in zip(parts, second_parts)]
    roots = [1.5 * second - 0.5 * mul(a, b) for second, a, b in zip(seconds, twice, scaled)]
    results = []
    for number, coupling in enumerate(couplings):
        left, right = roots[2 * number], roots[2 * number + 1]
        cross = mul(split(left), coupling)
        results.append((left, cross, cross.T, right))
    return results


def columns_kernel(parity, matrix, token, away, near, held, turned, loaded, stored):
    rows = matrix.shape[0]
    chunk = BLOCK
    loads = [
        pltpu.make_async_copy(matrix.at[pl.ds(k * chunk, chunk)], held.at[pl.ds(k * chunk, chunk)], loaded.at[k])
        for k in range(rows // chunk)
    ]
    for load in loads:
        load.start()
    left, cross, crossed, right = factors([token[...]])[0]
    even = parity[0] == 0
    first = jnp.concatenate([left, crossed], axis=0)
    second = jnp.concatenate([-cross, right], axis=0)
    turn = split(jnp.concatenate([jnp.where(even, first, second), jnp.where(even, second, first)], axis=1))
    stores = []
    for k in range(rows // chunk):
        here = pl.ds(k * chunk, chunk)
        loads[k].wait()
        turned[here, :] = mul(split(held[here, :]), turn)
        for half, target in enumerate((away, near)):
            store = pltpu.make_async_copy(
                turned.at[here, pl.ds(half * BLOCK, BLOCK)], target.at[here], stored.at[2 * k + half]
            )
            store.start()
            stores.append(store)
    for store in stores:
        store.wait()


def rotations_kernel(parity, mine, other, high, low):
    even = parity[0] == 0
    uppers = [jnp.where(even, mine[...], other[...]), jnp.where(even, other[...], mine[...])]
    for member, (left, cross, crossed, right) in enumerate(factors(uppers)):
        parts = split(
            jnp.concatenate(
                [jnp.concatenate([left, cross], axis=1), jnp.concatenate([-crossed, right], axis=1)], axis=0
            )
        )
        high[member], low[member] = parts


def gather_columns(chosen, sources, held, sems, pair, start):
    rows = pl.ds(pair * SPAN, SPAN)
    for half in range(2):
        for number, source in enumerate(sources):

            @pl.when(chosen[half] == number)
            def _():
                copy = pltpu.make_async_copy(
                    source.at[rows], held.at[rows, pl.ds(half * BLOCK, BLOCK)], sems.at[2 * pair + half]
                )
                copy.start() if start else copy.wait()


def edge_rows_kernel(chosen, s0, s1, s2, s3, high, low, send_a, send_b, held, edge, loaded, stored):
    sources = (s0, s1, s2, s3)
    for pair in range(2):
        gather_columns(chosen, sources, held, loaded, pair, True)
    for pair in range(2):
        gather_columns(chosen, sources, held, loaded, pair, False)
        lines = pl.ds(pair * BLOCK, BLOCK)
        edge[pair] = mul((high[pair, lines], low[pair, lines]), split(held[pl.ds(pair * SPAN, SPAN), :]))
        for even, target in ((pair == 1, send_a), (pair == 0, send_b)):

            @pl.when((chosen[2] == 0) == even)
            def _():
                pltpu.make_async_copy(edge.at[pair], target, stored.at[pair]).start()

    for pair in range(2):
        pltpu.make_async_copy(edge.at[pair], send_a, stored.at[pair]).wait()


def inner_rows_kernel(
    chosen, place, s0, s1, s2, s3, high, low, send_a, send_b, result, held, inside, loaded, stored
):
    sources = (s0, s1, s2, s3)
    for pair in range(2):
        gather_columns(chosen, sources, held, loaded, pair, True)
    for slot, source in ((0, send_b), (3, send_a)):
        for even, edge in ((True, source), (False, send_a if slot == 0 else send_b)):

            @pl.when((place[slot] >= 0) & ((chosen[2] == 0) == even))
            def _():
                spot = pl.multiple_of(place[slot] * BLOCK, BLOCK)
                pltpu.make_async_copy(edge, result.at[pl.ds(spot, BLOCK)], stored.at[slot]).start()

    for pair in range(2):
        gather_columns(chosen, sources, held, loaded, pair, False)
        lines = pl.ds((1 - pair) * BLOCK, BLOCK)
        inside[pair] = mul((high[pair, lines], low[pair, lines]), split(held[pl.ds(pair * SPAN, SPAN), :]))
        spot = pl.multiple_of(place[1 + pair] * BLOCK, BLOCK)
        pltpu.make_async_copy(inside.at[pair], result.at[pl.ds(spot, BLOCK)], stored.at[1 + pair]).start()
    for slot in range(4):

        @pl.when(place[slot] >= 0)
        def _():
            pltpu.make_async_copy(inside.at[0], result.at[pl.ds(0, BLOCK)], stored.at[slot]).wait()


def arrivals_kernel(place, got_a, got_b, partial, result, stored):
    del partial
    for number, got in enumerate((got_a, got_b)):

        @pl.when(place[number] >= 0)
        def _():
            spot = pl.multiple_of(place[number] * BLOCK, BLOCK)
            pltpu.make_async_copy(got, result.at[pl.ds(spot, BLOCK)], stored.at[number]).start()

    for number, got in enumerate((got_a, got_b)):

        @pl.when(place[number] >= 0)
        def _():
            pltpu.make_async_copy(got, result.at[pl.ds(0, BLOCK)], stored.at[number]).wait()


SMEM = pl.BlockSpec(memory_space=pltpu.SMEM)
VMEM = pl.BlockSpec(memory_space=pltpu.VMEM)
ANY = pl.BlockSpec(memory_space=pl.ANY)


def f32(*shape):
    return jax.ShapeDtypeStruct(shape, jnp.float32)


def call(kernel, out_shape, in_specs, out_specs, scratch, products, aliases=None):
    return pl.pallas_call(
        kernel,
        out_shape=out_shape,
        in_specs=in_specs,
        out_specs=out_specs,
        scratch_shapes=scratch,
        input_output_aliases=aliases or {},
        cost_estimate=pl.CostEstimate(
            flops=products * 3 * 2 * BLOCK**3, bytes_accessed=4 * 1024 * 1024, transcendentals=0
        ),
        compiler_params=pltpu.CompilerParams(vmem_limit_bytes=VMEM_LIMIT),
    )


def device(r, c):
    return r * 32 + c


def tree_pairs(sources, targets):
    pairs = []
    for c in range(32):
        z, h = c // 4, c // 2 % 2
        for (a, b), (d, e) in zip(sources, targets):
            pairs.append((device((z + a) % 8 * 2 + (h ^ b), c), device((z + d) % 8 * 2 + (h ^ e), c)))
    return pairs


def send(x, pairs):
    return lax.ppermute(x, AXES, pairs)


HOLDERS = [(0, 0), (4, 0), (2, 1), (6, 1)]
FIRST = [tree_pairs([(0, 0)], [target]) for target in HOLDERS[1:]]
SECOND = [
    tree_pairs(HOLDERS, [((z + step) % 8, h ^ flip) for z, h in HOLDERS]) for step, flip in ((0, 1), (1, 0), (7, 0))
]
TRANSPOSED = [(device(r, c), device(c // 2, 2 * r + c % 2)) for r in range(16) for c in range(32)]
CORES = [(device(r, c), device(r, c ^ 1)) for r in range(16) for c in range(32)]
CHIPS = [
    (device(r, c), device(r, d)) for r in range(16) for c in range(32) for d in [c - 1 + 2 * (c % 2)] if 0 <= d < 32
]
ROWS_A = [(device(r, c), device(r ^ 1, c)) for r in range(16) for c in range(32)]
ROWS_B = [
    (device(r, c), device(q, c)) for r in range(16) for c in range(32) for q in [r - 1 + 2 * (r % 2)] if 0 <= q < 16
]


def body(matrix, moves):
    r, c = lax.axis_index("row"), lax.axis_index("col")
    rows = matrix.shape[0]
    row_odd, col_odd = r % 2, c % 2
    order = moves[0]
    slots = jnp.arange(order.shape[0], dtype=jnp.int32)
    origin = jnp.sum(jnp.where(order[None, :] == slots[:, None], slots[None, :], 0), axis=1)

    upper = lax.dynamic_slice(matrix, (col_odd * SPAN, BLOCK), (BLOCK, BLOCK))
    token = jnp.where(r == c // 2, upper, sum(send(upper, pairs) for pairs in FIRST))
    token = token + sum(send(token, pairs) for pairs in SECOND)

    mine = send(token, TRANSPOSED)
    other = send(mine, CORES)

    parity = jnp.reshape(col_odd, (1,)).astype(jnp.int32)
    away, near = call(
        columns_kernel,
        (f32(rows, BLOCK), f32(rows, BLOCK)),
        [SMEM, ANY, VMEM],
        (ANY, ANY),
        [
            pltpu.VMEM((rows, SPAN), jnp.float32),
            pltpu.VMEM((rows, SPAN), jnp.float32),
            pltpu.SemaphoreType.DMA((rows // BLOCK,)),
            pltpu.SemaphoreType.DMA((2 * rows // BLOCK,)),
        ],
        13 + 16,
    )(parity, matrix, token)
    from_chip, from_core = send(away, CHIPS), send(near, CORES)

    half = jax.ShapeDtypeStruct((2, SPAN, SPAN), jnp.bfloat16)
    high, low = call(rotations_kernel, (half, half), [SMEM, VMEM, VMEM], (VMEM, VMEM), [], 26)(parity, mine, other)

    wanted = lax.dynamic_slice_in_dim(origin, 2 * c, 2) - 2 * c + 1
    table = jnp.where(col_odd == 0, jnp.array([2, 0, 1, 3]), jnp.array([3, 1, 0, 2])).astype(jnp.int32)
    chosen = jnp.concatenate([table[wanted], jnp.reshape(row_odd, (1,)).astype(jnp.int32)])
    columns = (away, near, from_chip, from_core)
    send_a, send_b = call(
        edge_rows_kernel,
        (f32(BLOCK, SPAN), f32(BLOCK, SPAN)),
        [SMEM] + [ANY] * 4 + [VMEM] * 2,
        (ANY, ANY),
        [
            pltpu.VMEM((rows, SPAN), jnp.float32),
            pltpu.VMEM((2, BLOCK, SPAN), jnp.float32),
            pltpu.SemaphoreType.DMA((4,)),
            pltpu.SemaphoreType.DMA((2,)),
        ],
        8,
    )(chosen, *columns, high, low)
    got_a, got_b = send(send_a, ROWS_A), send(send_b, ROWS_B)

    near_slots = 4 * r - 1 + jnp.arange(6, dtype=jnp.int32)
    known = (near_slots >= 0) & (near_slots < order.shape[0])
    target = order[jnp.clip(near_slots, 0, order.shape[0] - 1)] - 4 * r
    place = jnp.where(known & (target >= 0) & (target < 4), target, -1).astype(jnp.int32)
    partial = call(
        inner_rows_kernel,
        f32(rows, SPAN),
        [SMEM] * 2 + [ANY] * 4 + [VMEM] * 2 + [ANY] * 2,
        ANY,
        [
            pltpu.VMEM((rows, SPAN), jnp.float32),
            pltpu.VMEM((2, BLOCK, SPAN), jnp.float32),
            pltpu.SemaphoreType.DMA((4,)),
            pltpu.SemaphoreType.DMA((4,)),
        ],
        8,
    )(chosen, place[1:5], *columns, high, low, send_a, send_b)
    arrived = jnp.where(row_odd == 0, place[jnp.array([5, 0])], place[jnp.array([0, 5])])
    return call(
        arrivals_kernel,
        f32(rows, SPAN),
        [SMEM] + [ANY] * 3,
        ANY,
        [pltpu.SemaphoreType.DMA((2,))],
        0,
        aliases={3: 0},
    )(arrived, got_a, got_b, partial)


def solution(mesh):
    placed = (P("row", "col"), P())
    return jax.shard_map(body, mesh=mesh, in_specs=placed, out_specs=P("row", "col"), check_vma=False)
```

```python
import functools
import math

import jax
import jax.numpy as jnp
from jax import lax
from jax.experimental import pallas as pl
from jax.experimental.pallas import tpu as pltpu
from jax.sharding import PartitionSpec as P

BLOCK = 256
SPAN = 2 * BLOCK
AXES = ("row", "col")
VMEM_LIMIT = 32 * 1024 * 1024


def split(x):
    high = x.astype(jnp.bfloat16)
    low = (x - high.astype(jnp.float32)).astype(jnp.bfloat16)
    return high, low


def mul(a, b):
    dot = functools.partial(jnp.dot, preferred_element_type=jnp.float32)
    return dot(a[0], b[0]) + (dot(a[0], b[1]) + dot(a[1], b[0]))


def identity():
    rows = lax.broadcasted_iota(jnp.int32, (BLOCK, BLOCK), 0)
    columns = lax.broadcasted_iota(jnp.int32, (BLOCK, BLOCK), 1)
    return jnp.where(rows == columns, 1.0, 0.0).astype(jnp.float32)


def factors(uppers):
    eye = identity()
    first = 1.0 / math.sqrt(5.0)
    alpha, beta = 1.5 * first, -0.5 * first**3
    couplings, grams = [], []
    for upper in uppers:
        total = jnp.sum(jnp.sum(upper * upper, axis=1, keepdims=True), axis=0, keepdims=True)
        coupling = upper * lax.rsqrt(total / BLOCK + 1e-06)
        here, turned = split(coupling), split(coupling.T)
        couplings.append(here)
        grams.append(eye + mul(here, turned))
        grams.append(eye + mul(turned, here))
    parts = [split(gram) for gram in grams]
    squares = [mul(part, part) for part in parts]
    square_parts = [split(square) for square in squares]
    inner = [
        split(1.5 * alpha * beta**2 * gram + 0.5 * beta**3 * square) for gram, square in zip(grams, squares)
    ]
    seconds = [
        1.5 * alpha * eye + (1.5 * beta - 0.5 * alpha**3) * gram - 1.5 * alpha**2 * beta * square - mul(part, rest)
        for gram, square, part, rest in zip(grams, squares, square_parts, inner)
    ]
    second_parts = [split(second) for second in seconds]
    twice = [split(mul(part, part)) for part in second_parts]
    scaled = [split(mul(gram, part)) for gram, part in zip(parts, second_parts)]
    roots = [1.5 * second - 0.5 * mul(a, b) for second, a, b in zip(seconds, twice, scaled)]
    results = []
    for number, coupling in enumerate(couplings):
        left, right = roots[2 * number], roots[2 * number + 1]
        cross = mul(split(left), coupling)
        results.append((left, cross, cross.T, right))
    return results


def first_columns_kernel(matrix, token, away, near, high, low, held, loaded):
    load = pltpu.make_async_copy(matrix.at[pl.ds(0, SPAN)], held, loaded)
    load.start()
    left, cross, crossed, right = factors([token[...]])[0]
    even = lax.axis_index("col") % 2 == 0
    first = jnp.concatenate([left, crossed], axis=0)
    second = jnp.concatenate([-cross, right], axis=0)
    turn = split(jnp.concatenate([jnp.where(even, first, second), jnp.where(even, second, first)], axis=1))
    high[...], low[...] = turn
    load.wait()
    turned = mul(split(held[...]), turn)
    away[...] = turned[:, :BLOCK]
    near[...] = turned[:, BLOCK:]


def more_columns_kernel(matrix, high, low, away, near, held, loaded):
    load = pltpu.make_async_copy(matrix.at[pl.ds(SPAN, SPAN)], held, loaded)
    load.start()
    load.wait()
    turned = mul(split(held[...]), (high[...], low[...]))
    away[...] = turned[:, :BLOCK]
    near[...] = turned[:, BLOCK:]


def rotations_kernel(mine, other, high, low):
    even = lax.axis_index("col") % 2 == 0
    uppers = [jnp.where(even, mine[...], other[...]), jnp.where(even, other[...], mine[...])]
    for member, (left, cross, crossed, right) in enumerate(factors(uppers)):
        parts = split(
            jnp.concatenate(
                [jnp.concatenate([left, cross], axis=1), jnp.concatenate([-crossed, right], axis=1)], axis=0
            )
        )
        high[member], low[member] = parts


def rows_kernel(pair, moves, away, near, from_chip, from_core, high, low, upper, lower, held):
    c = lax.axis_index("col")
    odd = c % 2
    for slot, source in (
        (2 * c + odd, away),
        (2 * c + 1 - odd, near),
        (2 * c - 1 + 3 * odd, from_chip),
        (2 * c + 2 - 3 * odd, from_core),
    ):
        known = (slot >= 0) & (slot < moves.shape[1])
        target = moves[0, jnp.clip(slot, 0, moves.shape[1] - 1)] - 2 * c
        for half in range(2):

            @pl.when(known & (target == half))
            def _():
                held[:, half * BLOCK : (half + 1) * BLOCK] = source[...]

    turned = mul((high[pair], low[pair]), split(held[...]))
    upper[...] = turned[:BLOCK]
    lower[...] = turned[BLOCK:]


def place_kernel(moves, b0, b1, b2, b3, b4, b5, result, stored):
    r = lax.axis_index("row")

    def copies(act):
        for number, block in enumerate((b0, b1, b2, b3, b4, b5)):
            slot = 4 * r - 1 + number
            known = (slot >= 0) & (slot < moves.shape[1])
            target = moves[0, jnp.clip(slot, 0, moves.shape[1] - 1)] - 4 * r

            @pl.when(known & (target >= 0) & (target < 4))
            def _():
                spot = pl.multiple_of(jnp.clip(target, 0, 3) * BLOCK, BLOCK)
                act(pltpu.make_async_copy(block, result.at[pl.ds(spot, BLOCK)], stored.at[number]))

    copies(lambda copy: copy.start())
    copies(lambda copy: copy.wait())


SMEM = pl.BlockSpec(memory_space=pltpu.SMEM)
VMEM = pl.BlockSpec(memory_space=pltpu.VMEM)
HBM = pl.BlockSpec(memory_space=pltpu.HBM)


def f32(*shape):
    return jax.ShapeDtypeStruct(shape, jnp.float32)


def bf16(*shape):
    return jax.ShapeDtypeStruct(shape, jnp.bfloat16)


def call(kernel, out_shape, in_specs, out_specs, scratch, products):
    return pl.pallas_call(
        kernel,
        out_shape=out_shape,
        in_specs=in_specs,
        out_specs=out_specs,
        scratch_shapes=scratch,
        cost_estimate=pl.CostEstimate(
            flops=products * 3 * 2 * BLOCK**3, bytes_accessed=2 * 1024 * 1024, transcendentals=0
        ),
        compiler_params=pltpu.CompilerParams(vmem_limit_bytes=VMEM_LIMIT),
    )


def device(r, c):
    return r * 32 + c


def over_rows(sources, targets):
    pairs = []
    for c in range(32):
        z, h = c // 4, c // 2 % 2
        for (a, b), (d, e) in zip(sources, targets):
            pairs.append((device((z + a) % 8 * 2 + (h ^ b), c), device((z + d) % 8 * 2 + (h ^ e), c)))
    return pairs


def over_columns(sources, targets):
    pairs = []
    for r in range(16):
        for core in range(2):
            y, h = r // 2, r % 2
            for (a, b), (d, e) in zip(sources, targets):
                pairs.append(
                    (
                        device(r, (y + a) % 8 * 4 + (h ^ b) * 2 + core),
                        device(r, (y + d) % 8 * 4 + (h ^ e) * 2 + core),
                    )
                )
    return pairs


def send(x, pairs):
    return lax.ppermute(x, AXES, pairs)


HOLDERS = [(0, 0), (4, 0), (2, 1), (6, 1)]
STEPS = [(0, 1), (1, 0), (7, 0)]
NEXT = [[((z + step) % 8, h ^ flip) for z, h in HOLDERS] for step, flip in STEPS]
ROWS_1 = [over_rows([(0, 0)], [target]) for target in HOLDERS[1:]]
ROWS_2 = [over_rows(HOLDERS, targets) for targets in NEXT]
COLS_1 = [over_columns([(0, 0)], [target]) for target in HOLDERS[1:]]
COLS_2 = [over_columns(HOLDERS, targets) for targets in NEXT]
CORES = [(device(r, c), device(r, c ^ 1)) for r in range(16) for c in range(32)]
CHIPS = [
    (device(r, c), device(r, d)) for r in range(16) for c in range(32) for d in [c - 1 + 2 * (c % 2)] if 0 <= d < 32
]
UP = [(device(r, c), device(r - 1, c)) for r in range(1, 16) for c in range(32)]
DOWN = [(device(r, c), device(r + 1, c)) for r in range(15) for c in range(32)]


def body(matrix, moves):
    r, c = lax.axis_index("row"), lax.axis_index("col")

    upper = lax.dynamic_slice(matrix, ((c % 2) * SPAN, BLOCK), (BLOCK, BLOCK))
    owner = r == c // 2
    col_token = jnp.where(owner, upper, sum(send(upper, pairs) for pairs in ROWS_1))
    row_token = jnp.where(owner, upper, sum(send(upper, pairs) for pairs in COLS_1))
    col_token = col_token + sum(send(col_token, pairs) for pairs in ROWS_2)
    mine = row_token + sum(send(row_token, pairs) for pairs in COLS_2)
    other = send(mine, CORES)

    half = f32(SPAN, BLOCK)
    held = [pltpu.VMEM((SPAN, SPAN), jnp.float32), pltpu.SemaphoreType.DMA(())]
    away, near, high, low = call(
        first_columns_kernel,
        (half, half, bf16(SPAN, SPAN), bf16(SPAN, SPAN)),
        [HBM, VMEM],
        (VMEM,) * 4,
        held,
        13 + 8,
    )(matrix, col_token)
    parts = [(away, near, send(away, CHIPS), send(near, CORES))]
    away, near = call(more_columns_kernel, (half, half), [HBM, VMEM, VMEM], (VMEM,) * 2, held, 8)(matrix, high, low)
    parts.append((away, near, send(away, CHIPS), send(near, CORES)))

    high, low = call(rotations_kernel, (bf16(2, SPAN, SPAN),) * 2, [VMEM] * 2, (VMEM,) * 2, [], 26)(mine, other)
    wide = f32(BLOCK, SPAN)
    turn = [
        call(
            functools.partial(rows_kernel, pair),
            (wide, wide),
            [SMEM] + [VMEM] * 6,
            (VMEM,) * 2,
            [pltpu.VMEM((SPAN, SPAN), jnp.float32)],
            8,
        )
        for pair in range(2)
    ]
    first, second = turn[0](moves, *parts[0], high, low)
    below = send(first, UP)
    third, fourth = turn[1](moves, *parts[1], high, low)
    above = send(fourth, DOWN)
    return call(
        place_kernel, f32(*matrix.shape), [SMEM] + [VMEM] * 6, HBM, [pltpu.SemaphoreType.DMA((6,))], 0
    )(moves, above, first, second, third, fourth, below)


def solution(mesh):
    placed = (P("row", "col"), P())
    return jax.shard_map(body, mesh=mesh, in_specs=placed, out_specs=P("row", "col"), check_vma=False)
```

```python
import functools
import math

import jax
import jax.numpy as jnp
from jax import lax
from jax.experimental import pallas as pl
from jax.experimental.pallas import tpu as pltpu
from jax.sharding import PartitionSpec as P

BLOCK = 256
SPAN = 2 * BLOCK
AXES = ("row", "col")
VMEM_LIMIT = 32 * 1024 * 1024


def split(x):
    high = x.astype(jnp.bfloat16)
    low = (x - high.astype(jnp.float32)).astype(jnp.bfloat16)
    return high, low


def mul(a, b):
    dot = functools.partial(jnp.dot, preferred_element_type=jnp.float32)
    return dot(a[0], b[0]) + (dot(a[0], b[1]) + dot(a[1], b[0]))


def identity():
    rows = lax.broadcasted_iota(jnp.int32, (BLOCK, BLOCK), 0)
    columns = lax.broadcasted_iota(jnp.int32, (BLOCK, BLOCK), 1)
    return jnp.where(rows == columns, 1.0, 0.0).astype(jnp.float32)


def factors(uppers):
    eye = identity()
    first = 1.0 / math.sqrt(5.0)
    alpha, beta = 1.5 * first, -0.5 * first**3
    couplings, grams = [], []
    for upper in uppers:
        total = jnp.sum(jnp.sum(upper * upper, axis=1, keepdims=True), axis=0, keepdims=True)
        coupling = upper * lax.rsqrt(total / BLOCK + 1e-06)
        here, turned = split(coupling), split(coupling.T)
        couplings.append(here)
        grams.append(eye + mul(here, turned))
        grams.append(eye + mul(turned, here))
    parts = [split(gram) for gram in grams]
    squares = [mul(part, part) for part in parts]
    square_parts = [split(square) for square in squares]
    inner = [
        split(1.5 * alpha * beta**2 * gram + 0.5 * beta**3 * square) for gram, square in zip(grams, squares)
    ]
    seconds = [
        1.5 * alpha * eye + (1.5 * beta - 0.5 * alpha**3) * gram - 1.5 * alpha**2 * beta * square - mul(part, rest)
        for gram, square, part, rest in zip(grams, squares, square_parts, inner)
    ]
    second_parts = [split(second) for second in seconds]
    twice = [split(mul(part, part)) for part in second_parts]
    scaled = [split(mul(gram, part)) for gram, part in zip(parts, second_parts)]
    roots = [1.5 * second - 0.5 * mul(a, b) for second, a, b in zip(seconds, twice, scaled)]
    results = []
    for number, coupling in enumerate(couplings):
        left, right = roots[2 * number], roots[2 * number + 1]
        cross = mul(split(left), coupling)
        results.append((left, cross, cross.T, right))
    return results


def pivot_kernel(matrix, upper, loaded):
    first = pl.multiple_of(lax.axis_index("col") % 2 * SPAN, SPAN)
    load = pltpu.make_async_copy(matrix.at[pl.ds(first, BLOCK), pl.ds(BLOCK, BLOCK)], upper, loaded)
    load.start()
    load.wait()


def again_kernel(upper, copy):
    copy[...] = upper[...]


def join_kernel(first, t0, t1, t2, token):
    owner = lax.axis_index("row") == lax.axis_index("col") // 2
    token[...] = jnp.where(owner, first[...], t0[...] + (t1[...] + t2[...]))


def sum_kernel(first, t0, t1, t2, token):
    token[...] = (first[...] + t0[...]) + (t1[...] + t2[...])


def first_columns_kernel(matrix, t0, t1, t2, t3, away, near, high, low, held, loaded):
    load = pltpu.make_async_copy(matrix.at[pl.ds(0, SPAN)], held, loaded)
    load.start()
    left, cross, crossed, right = factors([t0[...] + ((t1[...] + t2[...]) + t3[...])])[0]
    even = lax.axis_index("col") % 2 == 0
    first = jnp.concatenate([left, crossed], axis=0)
    second = jnp.concatenate([-cross, right], axis=0)
    turn = split(jnp.concatenate([jnp.where(even, first, second), jnp.where(even, second, first)], axis=1))
    high[...], low[...] = turn
    load.wait()
    turned = mul(split(held[...]), turn)
    away[...] = turned[:, :BLOCK]
    near[...] = turned[:, BLOCK:]


def more_columns_kernel(matrix, high, low, away, near, held, loaded):
    load = pltpu.make_async_copy(matrix.at[pl.ds(SPAN, SPAN)], held, loaded)
    load.start()
    load.wait()
    turned = mul(split(held[...]), (high[...], low[...]))
    away[...] = turned[:, :BLOCK]
    near[...] = turned[:, BLOCK:]


def rotations_kernel(mine, other, high, low):
    even = lax.axis_index("col") % 2 == 0
    uppers = [jnp.where(even, mine[...], other[...]), jnp.where(even, other[...], mine[...])]
    for member, (left, cross, crossed, right) in enumerate(factors(uppers)):
        parts = split(
            jnp.concatenate(
                [jnp.concatenate([left, cross], axis=1), jnp.concatenate([-crossed, right], axis=1)], axis=0
            )
        )
        high[member], low[member] = parts


def rows_kernel(pair, moves, away, near, from_chip, from_core, high, low, upper, lower, held):
    c = lax.axis_index("col")
    odd = c % 2
    for slot, source in (
        (2 * c + odd, away),
        (2 * c + 1 - odd, near),
        (2 * c - 1 + 3 * odd, from_chip),
        (2 * c + 2 - 3 * odd, from_core),
    ):
        known = (slot >= 0) & (slot < moves.shape[1])
        target = moves[0, jnp.clip(slot, 0, moves.shape[1] - 1)] - 2 * c
        for half in range(2):

            @pl.when(known & (target == half))
            def _():
                held[:, half * BLOCK : (half + 1) * BLOCK] = source[...]

    turned = mul((high[pair], low[pair]), split(held[...]))
    upper[...] = turned[:BLOCK]
    lower[...] = turned[BLOCK:]


def place_kernel(moves, b0, b1, b2, b3, b4, b5, result, stored):
    r = lax.axis_index("row")

    def copies(act):
        for number, block in enumerate((b0, b1, b2, b3, b4, b5)):
            slot = 4 * r - 1 + number
            known = (slot >= 0) & (slot < moves.shape[1])
            target = moves[0, jnp.clip(slot, 0, moves.shape[1] - 1)] - 4 * r

            @pl.when(known & (target >= 0) & (target < 4))
            def _():
                spot = pl.multiple_of(jnp.clip(target, 0, 3) * BLOCK, BLOCK)
                act(pltpu.make_async_copy(block, result.at[pl.ds(spot, BLOCK)], stored.at[number]))

    copies(lambda copy: copy.start())
    copies(lambda copy: copy.wait())


SMEM = pl.BlockSpec(memory_space=pltpu.SMEM)
VMEM = pl.BlockSpec(memory_space=pltpu.VMEM)
HBM = pl.BlockSpec(memory_space=pltpu.HBM)


def f32(*shape):
    return jax.ShapeDtypeStruct(shape, jnp.float32)


def bf16(*shape):
    return jax.ShapeDtypeStruct(shape, jnp.bfloat16)


def call(kernel, out_shape, in_specs, out_specs, scratch, products):
    return pl.pallas_call(
        kernel,
        out_shape=out_shape,
        in_specs=in_specs,
        out_specs=out_specs,
        scratch_shapes=scratch,
        cost_estimate=pl.CostEstimate(
            flops=products * 3 * 2 * BLOCK**3, bytes_accessed=0, transcendentals=0
        ),
        compiler_params=pltpu.CompilerParams(vmem_limit_bytes=VMEM_LIMIT),
    )


def device(r, c):
    return r * 32 + c


def over_rows(sources, targets):
    pairs = []
    for c in range(32):
        z, h = c // 4, c // 2 % 2
        for (a, b), (d, e) in zip(sources, targets):
            pairs.append((device((z + a) % 8 * 2 + (h ^ b), c), device((z + d) % 8 * 2 + (h ^ e), c)))
    return pairs


def over_columns(sources, targets):
    pairs = []
    for r in range(16):
        for core in range(2):
            y, h = r // 2, r % 2
            for (a, b), (d, e) in zip(sources, targets):
                pairs.append(
                    (
                        device(r, (y + a) % 8 * 4 + (h ^ b) * 2 + core),
                        device(r, (y + d) % 8 * 4 + (h ^ e) * 2 + core),
                    )
                )
    return pairs


def send(x, pairs):
    return lax.ppermute(x, AXES, pairs)


HOLDERS = [(0, 0), (4, 0), (2, 1), (6, 1)]
STEPS = [(0, 1), (1, 0), (7, 0)]
ROWS_1 = [over_rows([(0, 0)], [target]) for target in HOLDERS[1:]]
ROWS_2 = [over_rows(HOLDERS, [((z + step) % 8, h ^ flip) for z, h in HOLDERS]) for step, flip in STEPS]
EVEN = [(0, 0), (4, 0), (2, 0), (6, 0)]
COLS_1 = [over_columns([(0, 0)], [target]) for target in EVEN[1:]]
COLS_2 = [over_columns(EVEN, [((y + step) % 8, flip) for y, _ in EVEN]) for step, flip in ((1, 0), (0, 1), (1, 1))]
CORES = [(device(r, c), device(r, c ^ 1)) for r in range(16) for c in range(32)]
CHIPS = [
    (device(r, c), device(r, d)) for r in range(16) for c in range(32) for d in [c - 1 + 2 * (c % 2)] if 0 <= d < 32
]
UP = [(device(r, c), device(r - 1, c)) for r in range(1, 16) for c in range(32)]
DOWN = [(device(r, c), device(r + 1, c)) for r in range(15) for c in range(32)]


def body(matrix, moves):
    upper = call(
        pivot_kernel, f32(BLOCK, BLOCK), [HBM], VMEM, [pltpu.SemaphoreType.DMA(())], 0
    )(matrix)
    again = call(again_kernel, f32(BLOCK, BLOCK), [VMEM], VMEM, [], 0)(upper)
    join = call(join_kernel, f32(BLOCK, BLOCK), [VMEM] * 4, VMEM, [], 0)
    col_token = join(upper, *[send(upper, pairs) for pairs in ROWS_1])
    col_tokens = [col_token] + [send(col_token, pairs) for pairs in ROWS_2]
    row_token = join(again, *[send(again, pairs) for pairs in COLS_1])
    mine = call(sum_kernel, f32(BLOCK, BLOCK), [VMEM] * 4, VMEM, [], 0)(
        row_token, *[send(row_token, pairs) for pairs in COLS_2]
    )
    other = send(mine, CORES)

    half = f32(SPAN, BLOCK)
    held = [pltpu.VMEM((SPAN, SPAN), jnp.float32), pltpu.SemaphoreType.DMA(())]
    away, near, high, low = call(
        first_columns_kernel,
        (half, half, bf16(SPAN, SPAN), bf16(SPAN, SPAN)),
        [HBM] + [VMEM] * 4,
        (VMEM,) * 4,
        held,
        0,
    )(matrix, *col_tokens)
    parts = [(away, near, send(away, CHIPS), send(near, CORES))]
    away, near = call(more_columns_kernel, (half, half), [HBM, VMEM, VMEM], (VMEM,) * 2, held, 0)(matrix, high, low)
    parts.append((away, near, send(away, CHIPS), send(near, CORES)))

    high, low = call(rotations_kernel, (bf16(2, SPAN, SPAN),) * 2, [VMEM] * 2, (VMEM,) * 2, [], 0)(mine, other)
    wide = f32(BLOCK, SPAN)
    turn = [
        call(
            functools.partial(rows_kernel, pair),
            (wide, wide),
            [SMEM] + [VMEM] * 6,
            (VMEM,) * 2,
            [pltpu.VMEM((SPAN, SPAN), jnp.float32)],
            0,
        )
        for pair in range(2)
    ]
    first, second = turn[0](moves, *parts[0], high, low)
    below = send(first, UP)
    third, fourth = turn[1](moves, *parts[1], high, low)
    above = send(fourth, DOWN)
    return call(
        place_kernel, f32(*matrix.shape), [SMEM] + [VMEM] * 6, HBM, [pltpu.SemaphoreType.DMA((6,))], 0
    )(moves, above, first, second, third, fourth, below)


def solution(mesh):
    placed = (P("row", "col"), P())
    return jax.shard_map(body, mesh=mesh, in_specs=placed, out_specs=P("row", "col"), check_vma=False)
```

```python
import functools
import math

import jax
import jax.numpy as jnp
from jax import lax
from jax.experimental import pallas as pl
from jax.experimental.pallas import tpu as pltpu
from jax.sharding import PartitionSpec as P

BLOCK = 256
SPAN = 2 * BLOCK
AXES = ("row", "col")
VMEM_LIMIT = 32 * 1024 * 1024


def split(x):
    high = x.astype(jnp.bfloat16)
    low = (x - high.astype(jnp.float32)).astype(jnp.bfloat16)
    return high, low


def mul(a, b):
    dot = functools.partial(jnp.dot, preferred_element_type=jnp.float32)
    return dot(a[0], b[0]) + (dot(a[0], b[1]) + dot(a[1], b[0]))


def identity():
    rows = lax.broadcasted_iota(jnp.int32, (BLOCK, BLOCK), 0)
    columns = lax.broadcasted_iota(jnp.int32, (BLOCK, BLOCK), 1)
    return jnp.where(rows == columns, 1.0, 0.0).astype(jnp.float32)


def factors(uppers):
    eye = identity()
    first = 1.0 / math.sqrt(5.0)
    alpha, beta = 1.5 * first, -0.5 * first**3
    couplings, grams = [], []
    for upper in uppers:
        total = jnp.sum(jnp.sum(upper * upper, axis=1, keepdims=True), axis=0, keepdims=True)
        coupling = upper * lax.rsqrt(total / BLOCK + 1e-06)
        here, turned = split(coupling), split(coupling.T)
        couplings.append(here)
        grams.append(eye + mul(here, turned))
        grams.append(eye + mul(turned, here))
    parts = [split(gram) for gram in grams]
    squares = [mul(part, part) for part in parts]
    square_parts = [split(square) for square in squares]
    inner = [
        split(1.5 * alpha * beta**2 * gram + 0.5 * beta**3 * square) for gram, square in zip(grams, squares)
    ]
    seconds = [
        1.5 * alpha * eye + (1.5 * beta - 0.5 * alpha**3) * gram - 1.5 * alpha**2 * beta * square - mul(part, rest)
        for gram, square, part, rest in zip(grams, squares, square_parts, inner)
    ]
    second_parts = [split(second) for second in seconds]
    twice = [split(mul(part, part)) for part in second_parts]
    scaled = [split(mul(gram, part)) for gram, part in zip(parts, second_parts)]
    roots = [1.5 * second - 0.5 * mul(a, b) for second, a, b in zip(seconds, twice, scaled)]
    results = []
    for number, coupling in enumerate(couplings):
        left, right = roots[2 * number], roots[2 * number + 1]
        cross = mul(split(left), coupling)
        results.append((left, cross, cross.T, right))
    return results


def again_kernel(upper, copy):
    copy[...] = upper[...]


def join_kernel(first, t0, t1, t2, token):
    owner = lax.axis_index("row") == lax.axis_index("col") // 2
    token[...] = jnp.where(owner, first[...], t0[...] + (t1[...] + t2[...]))


def sum_kernel(first, t0, t1, t2, token):
    token[...] = (first[...] + t0[...]) + (t1[...] + t2[...])


def first_columns_kernel(matrix, t0, t1, t2, t3, away, near, high, low, held, loaded):
    load = pltpu.make_async_copy(matrix.at[pl.ds(0, SPAN)], held, loaded)
    load.start()
    left, cross, crossed, right = factors([t0[...] + ((t1[...] + t2[...]) + t3[...])])[0]
    even = lax.axis_index("col") % 2 == 0
    first = jnp.concatenate([left, crossed], axis=0)
    second = jnp.concatenate([-cross, right], axis=0)
    turn = split(jnp.concatenate([jnp.where(even, first, second), jnp.where(even, second, first)], axis=1))
    high[...], low[...] = turn
    load.wait()
    turned = mul(split(held[...]), turn)
    away[...] = turned[:, :BLOCK]
    near[...] = turned[:, BLOCK:]


def more_columns_kernel(matrix, high, low, away, near, held, loaded):
    load = pltpu.make_async_copy(matrix.at[pl.ds(SPAN, SPAN)], held, loaded)
    load.start()
    load.wait()
    turned = mul(split(held[...]), (high[...], low[...]))
    away[...] = turned[:, :BLOCK]
    near[...] = turned[:, BLOCK:]


def rotations_kernel(mine, other, high, low):
    even = lax.axis_index("col") % 2 == 0
    uppers = [jnp.where(even, mine[...], other[...]), jnp.where(even, other[...], mine[...])]
    for member, (left, cross, crossed, right) in enumerate(factors(uppers)):
        parts = split(
            jnp.concatenate(
                [jnp.concatenate([left, cross], axis=1), jnp.concatenate([-crossed, right], axis=1)], axis=0
            )
        )
        high[member], low[member] = parts


def rows_kernel(pair, moves, away, near, from_chip, from_core, high, low, upper, lower, held):
    c = lax.axis_index("col")
    odd = c % 2
    for slot, source in (
        (2 * c + odd, away),
        (2 * c + 1 - odd, near),
        (2 * c - 1 + 3 * odd, from_chip),
        (2 * c + 2 - 3 * odd, from_core),
    ):
        known = (slot >= 0) & (slot < moves.shape[1])
        target = moves[0, jnp.clip(slot, 0, moves.shape[1] - 1)] - 2 * c
        for half in range(2):

            @pl.when(known & (target == half))
            def _():
                held[:, half * BLOCK : (half + 1) * BLOCK] = source[...]

    turned = mul((high[pair], low[pair]), split(held[...]))
    upper[...] = turned[:BLOCK]
    lower[...] = turned[BLOCK:]


def place_blocks(offsets, moves, blocks, result, stored):
    r = lax.axis_index("row")

    def copies(act):
        for number, (offset, block) in enumerate(zip(offsets, blocks)):
            slot = 4 * r + offset
            known = (slot >= 0) & (slot < moves.shape[1])
            target = moves[0, jnp.clip(slot, 0, moves.shape[1] - 1)] - 4 * r

            @pl.when(known & (target >= 0) & (target < 4))
            def _():
                spot = pl.multiple_of(jnp.clip(target, 0, 3) * BLOCK, BLOCK)
                act(pltpu.make_async_copy(block, result.at[pl.ds(spot, BLOCK)], stored.at[number]))

    copies(lambda copy: copy.start())
    copies(lambda copy: copy.wait())


def own_kernel(moves, b0, b1, b2, b3, result, stored):
    place_blocks((0, 1, 2, 3), moves, (b0, b1, b2, b3), result, stored)


def arrivals_kernel(moves, above, below, partial, result, stored):
    del partial
    place_blocks((-1, 4), moves, (above, below), result, stored)


SMEM = pl.BlockSpec(memory_space=pltpu.SMEM)
VMEM = pl.BlockSpec(memory_space=pltpu.VMEM)
HBM = pl.BlockSpec(memory_space=pltpu.HBM)


def f32(*shape):
    return jax.ShapeDtypeStruct(shape, jnp.float32)


def bf16(*shape):
    return jax.ShapeDtypeStruct(shape, jnp.bfloat16)


def call(kernel, out_shape, in_specs, out_specs, scratch, products, aliases=None):
    return pl.pallas_call(
        kernel,
        out_shape=out_shape,
        in_specs=in_specs,
        out_specs=out_specs,
        scratch_shapes=scratch,
        input_output_aliases=aliases or {},
        cost_estimate=pl.CostEstimate(
            flops=products * 3 * 2 * BLOCK**3, bytes_accessed=0, transcendentals=0
        ),
        compiler_params=pltpu.CompilerParams(vmem_limit_bytes=VMEM_LIMIT),
    )


def device(r, c):
    return r * 32 + c


def over_rows(sources, targets):
    pairs = []
    for c in range(32):
        z, h = c // 4, c // 2 % 2
        for (a, b), (d, e) in zip(sources, targets):
            pairs.append((device((z + a) % 8 * 2 + (h ^ b), c), device((z + d) % 8 * 2 + (h ^ e), c)))
    return pairs


def over_columns(sources, targets):
    pairs = []
    for r in range(16):
        for core in range(2):
            y, h = r // 2, r % 2
            for (a, b), (d, e) in zip(sources, targets):
                pairs.append(
                    (
                        device(r, (y + a) % 8 * 4 + (h ^ b) * 2 + core),
                        device(r, (y + d) % 8 * 4 + (h ^ e) * 2 + core),
                    )
                )
    return pairs


def send(x, pairs):
    return lax.ppermute(x, AXES, pairs)


HOLDERS = [(0, 0), (4, 0), (2, 1), (6, 1)]
STEPS = [(0, 1), (1, 0), (7, 0)]
ROWS_1 = [over_rows([(0, 0)], [target]) for target in HOLDERS[1:]]
ROWS_2 = [over_rows(HOLDERS, [((z + step) % 8, h ^ flip) for z, h in HOLDERS]) for step, flip in STEPS]
EVEN = [(0, 0), (4, 0), (2, 0), (6, 0)]
COLS_1 = [over_columns([(0, 0)], [target]) for target in EVEN[1:]]
COLS_2 = [over_columns(EVEN, [((y + step) % 8, flip) for y, _ in EVEN]) for step, flip in ((1, 0), (0, 1), (1, 1))]
CORES = [(device(r, c), device(r, c ^ 1)) for r in range(16) for c in range(32)]
CHIPS = [
    (device(r, c), device(r, d)) for r in range(16) for c in range(32) for d in [c - 1 + 2 * (c % 2)] if 0 <= d < 32
]
UP = [(device(r, c), device(r - 1, c)) for r in range(1, 16) for c in range(32)]
DOWN = [(device(r, c), device(r + 1, c)) for r in range(15) for c in range(32)]


def body(matrix, moves):
    odd = lax.axis_index("col") % 2
    upper = lax.dynamic_slice(matrix, (odd * SPAN, BLOCK), (BLOCK, BLOCK))
    again = call(again_kernel, f32(BLOCK, BLOCK), [VMEM], VMEM, [], 0)(upper)
    join = call(join_kernel, f32(BLOCK, BLOCK), [VMEM] * 4, VMEM, [], 0)
    col_token = join(upper, *[send(upper, pairs) for pairs in ROWS_1])
    col_tokens = [col_token] + [send(col_token, pairs) for pairs in ROWS_2]
    row_token = join(again, *[send(again, pairs) for pairs in COLS_1])
    mine = call(sum_kernel, f32(BLOCK, BLOCK), [VMEM] * 4, VMEM, [], 0)(
        row_token, *[send(row_token, pairs) for pairs in COLS_2]
    )
    other = send(mine, CORES)

    half = f32(SPAN, BLOCK)
    held = [pltpu.VMEM((SPAN, SPAN), jnp.float32), pltpu.SemaphoreType.DMA(())]
    away, near, high, low = call(
        first_columns_kernel,
        (half, half, bf16(SPAN, SPAN), bf16(SPAN, SPAN)),
        [HBM] + [VMEM] * 4,
        (VMEM,) * 4,
        held,
        0,
    )(matrix, *col_tokens)
    parts = [(away, near, send(away, CHIPS), send(near, CORES))]
    away, near = call(more_columns_kernel, (half, half), [HBM, VMEM, VMEM], (VMEM,) * 2, held, 0)(matrix, high, low)
    parts.append((away, near, send(away, CHIPS), send(near, CORES)))

    high, low = call(rotations_kernel, (bf16(2, SPAN, SPAN),) * 2, [VMEM] * 2, (VMEM,) * 2, [], 0)(mine, other)
    wide = f32(BLOCK, SPAN)
    turn = [
        call(
            functools.partial(rows_kernel, pair),
            (wide, wide),
            [SMEM] + [VMEM] * 6,
            (VMEM,) * 2,
            [pltpu.VMEM((SPAN, SPAN), jnp.float32)],
            0,
        )
        for pair in range(2)
    ]
    first, second = turn[0](moves, *parts[0], high, low)
    below = send(first, UP)
    third, fourth = turn[1](moves, *parts[1], high, low)
    above = send(fourth, DOWN)
    partial = call(
        own_kernel, f32(*matrix.shape), [SMEM] + [VMEM] * 4, HBM, [pltpu.SemaphoreType.DMA((4,))], 0
    )(moves, first, second, third, fourth)
    return call(
        arrivals_kernel,
        f32(*matrix.shape),
        [SMEM] + [VMEM] * 2 + [HBM],
        HBM,
        [pltpu.SemaphoreType.DMA((2,))],
        0,
        aliases={3: 0},
    )(moves, above, below, partial)


def solution(mesh):
    placed = (P("row", "col"), P())
    return jax.shard_map(body, mesh=mesh, in_specs=placed, out_specs=P("row", "col"), check_vma=False)
```

```python
import functools
import math

import jax
import jax.numpy as jnp
from jax import lax
from jax.experimental import pallas as pl
from jax.experimental.pallas import tpu as pltpu
from jax.sharding import PartitionSpec as P

BLOCK = 256
SPAN = 2 * BLOCK
AXES = ("row", "col")
VMEM_LIMIT = 32 * 1024 * 1024


def split(x):
    high = x.astype(jnp.bfloat16)
    low = (x - high.astype(jnp.float32)).astype(jnp.bfloat16)
    return high, low


def mul(a, b):
    dot = functools.partial(jnp.dot, preferred_element_type=jnp.float32)
    return dot(a[0], b[0]) + (dot(a[0], b[1]) + dot(a[1], b[0]))


def identity():
    rows = lax.broadcasted_iota(jnp.int32, (BLOCK, BLOCK), 0)
    columns = lax.broadcasted_iota(jnp.int32, (BLOCK, BLOCK), 1)
    return jnp.where(rows == columns, 1.0, 0.0).astype(jnp.float32)


def factors(uppers):
    eye = identity()
    first = 1.0 / math.sqrt(5.0)
    alpha, beta = 1.5 * first, -0.5 * first**3
    couplings, grams = [], []
    for upper in uppers:
        total = jnp.sum(jnp.sum(upper * upper, axis=1, keepdims=True), axis=0, keepdims=True)
        coupling = upper * lax.rsqrt(total / BLOCK + 1e-06)
        here, turned = split(coupling), split(coupling.T)
        couplings.append(here)
        grams.append(eye + mul(here, turned))
        grams.append(eye + mul(turned, here))
    parts = [split(gram) for gram in grams]
    squares = [mul(part, part) for part in parts]
    square_parts = [split(square) for square in squares]
    inner = [
        split(1.5 * alpha * beta**2 * gram + 0.5 * beta**3 * square) for gram, square in zip(grams, squares)
    ]
    seconds = [
        1.5 * alpha * eye + (1.5 * beta - 0.5 * alpha**3) * gram - 1.5 * alpha**2 * beta * square - mul(part, rest)
        for gram, square, part, rest in zip(grams, squares, square_parts, inner)
    ]
    second_parts = [split(second) for second in seconds]
    twice = [split(mul(part, part)) for part in second_parts]
    scaled = [split(mul(gram, part)) for gram, part in zip(parts, second_parts)]
    roots = [1.5 * second - 0.5 * mul(a, b) for second, a, b in zip(seconds, twice, scaled)]
    results = []
    for number, coupling in enumerate(couplings):
        left, right = roots[2 * number], roots[2 * number + 1]
        cross = mul(split(left), coupling)
        results.append((left, cross, cross.T, right))
    return results


def again_kernel(upper, copy):
    copy[...] = upper[...]


def join_kernel(first, t0, t1, t2, token):
    owner = lax.axis_index("row") == lax.axis_index("col") // 2
    token[...] = jnp.where(owner, first[...], t0[...] + (t1[...] + t2[...]))


def sum_kernel(first, t0, t1, t2, token):
    token[...] = (first[...] + t0[...]) + (t1[...] + t2[...])


def first_columns_kernel(matrix, t0, t1, t2, t3, away, near, high, low, held, loaded):
    load = pltpu.make_async_copy(matrix.at[pl.ds(0, SPAN)], held, loaded)
    load.start()
    left, cross, crossed, right = factors([t0[...] + ((t1[...] + t2[...]) + t3[...])])[0]
    even = lax.axis_index("col") % 2 == 0
    first = jnp.concatenate([left, crossed], axis=0)
    second = jnp.concatenate([-cross, right], axis=0)
    turn = split(jnp.concatenate([jnp.where(even, first, second), jnp.where(even, second, first)], axis=1))
    high[...], low[...] = turn
    load.wait()
    turned = mul(split(held[...]), turn)
    away[...] = turned[:, :BLOCK]
    near[...] = turned[:, BLOCK:]


def more_columns_kernel(matrix, high, low, away, near, held, loaded):
    load = pltpu.make_async_copy(matrix.at[pl.ds(SPAN, SPAN)], held, loaded)
    load.start()
    load.wait()
    turned = mul(split(held[...]), (high[...], low[...]))
    away[...] = turned[:, :BLOCK]
    near[...] = turned[:, BLOCK:]


def rotations_kernel(mine, other, high, low):
    even = lax.axis_index("col") % 2 == 0
    uppers = [jnp.where(even, mine[...], other[...]), jnp.where(even, other[...], mine[...])]
    for member, (left, cross, crossed, right) in enumerate(factors(uppers)):
        parts = split(
            jnp.concatenate(
                [jnp.concatenate([left, cross], axis=1), jnp.concatenate([-crossed, right], axis=1)], axis=0
            )
        )
        high[member], low[member] = parts


def rows_kernel(pair, moves, away, near, from_chip, from_core, high, low, upper, lower, held):
    c = lax.axis_index("col")
    odd = c % 2
    for slot, source in (
        (2 * c + odd, away),
        (2 * c + 1 - odd, near),
        (2 * c - 1 + 3 * odd, from_chip),
        (2 * c + 2 - 3 * odd, from_core),
    ):
        known = (slot >= 0) & (slot < moves.shape[1])
        target = moves[0, jnp.clip(slot, 0, moves.shape[1] - 1)] - 2 * c
        for half in range(2):

            @pl.when(known & (target == half))
            def _():
                held[:, half * BLOCK : (half + 1) * BLOCK] = source[...]

    turned = mul((high[pair], low[pair]), split(held[...]))
    upper[...] = turned[:BLOCK]
    lower[...] = turned[BLOCK:]


def place_blocks(offsets, moves, blocks, result, stored):
    r = lax.axis_index("row")

    def copies(act):
        for number, (offset, block) in enumerate(zip(offsets, blocks)):
            slot = 4 * r + offset
            known = (slot >= 0) & (slot < moves.shape[1])
            target = moves[0, jnp.clip(slot, 0, moves.shape[1] - 1)] - 4 * r

            @pl.when(known & (target >= 0) & (target < 4))
            def _():
                spot = pl.multiple_of(jnp.clip(target, 0, 3) * BLOCK, BLOCK)
                act(pltpu.make_async_copy(block, result.at[pl.ds(spot, BLOCK)], stored.at[number]))

    copies(lambda copy: copy.start())
    copies(lambda copy: copy.wait())


def own_kernel(moves, b0, b1, b2, b3, result, stored):
    place_blocks((0, 1, 2, 3), moves, (b0, b1, b2, b3), result, stored)


def arrivals_kernel(moves, above, below, partial, result, stored):
    del partial
    place_blocks((-1, 4), moves, (above, below), result, stored)


SMEM = pl.BlockSpec(memory_space=pltpu.SMEM)
VMEM = pl.BlockSpec(memory_space=pltpu.VMEM)
HBM = pl.BlockSpec(memory_space=pltpu.HBM)


def f32(*shape):
    return jax.ShapeDtypeStruct(shape, jnp.float32)


def bf16(*shape):
    return jax.ShapeDtypeStruct(shape, jnp.bfloat16)


def call(kernel, out_shape, in_specs, out_specs, scratch, products, aliases=None):
    return pl.pallas_call(
        kernel,
        out_shape=out_shape,
        in_specs=in_specs,
        out_specs=out_specs,
        scratch_shapes=scratch,
        input_output_aliases=aliases or {},
        cost_estimate=pl.CostEstimate(
            flops=products * 3 * 2 * BLOCK**3, bytes_accessed=0, transcendentals=0
        ),
        compiler_params=pltpu.CompilerParams(vmem_limit_bytes=VMEM_LIMIT),
    )


def device(r, c):
    return r * 32 + c


def over_rows(sources, targets):
    pairs = []
    for c in range(32):
        z, h = c // 4, c // 2 % 2
        for (a, b), (d, e) in zip(sources, targets):
            pairs.append((device((z + a) % 8 * 2 + (h ^ b), c), device((z + d) % 8 * 2 + (h ^ e), c)))
    return pairs


def over_columns(sources, targets):
    pairs = []
    for r in range(16):
        for core in range(2):
            y, h = r // 2, r % 2
            for (a, b), (d, e) in zip(sources, targets):
                pairs.append(
                    (
                        device(r, (y + a) % 8 * 4 + (h ^ b) * 2 + core),
                        device(r, (y + d) % 8 * 4 + (h ^ e) * 2 + core),
                    )
                )
    return pairs


def send(x, pairs):
    return lax.ppermute(x, AXES, pairs)


HOLDERS = [(0, 0), (4, 0), (2, 1), (6, 1)]
STEPS = [(0, 1), (1, 0), (7, 0)]
FIRST = [(0, 0), (2, 0), (6, 0), (4, 1)]
ROWS_1 = [over_rows([(0, 0)], [target]) for target in FIRST[1:]]
ROWS_2 = [
    over_rows(FIRST, targets)
    for targets in (
        [(0, 1), (2, 1), (6, 1), (4, 0)],
        [(1, 0), (3, 0), (5, 0), (3, 1)],
        [(7, 0), (1, 1), (7, 1), (5, 1)],
    )
]
COLS_1 = [over_columns([(0, 0)], [target]) for target in HOLDERS[1:]]
COLS_2 = [
    over_columns(HOLDERS, targets)
    for targets in (
        [(1, 0), (3, 0), (1, 1), (5, 1)],
        [(7, 0), (5, 0), (3, 1), (7, 1)],
        [(2, 0), (6, 0), (0, 1), (4, 1)],
    )
]
CORES = [(device(r, c), device(r, c ^ 1)) for r in range(16) for c in range(32)]
CHIPS = [
    (device(r, c), device(r, d)) for r in range(16) for c in range(32) for d in [c - 1 + 2 * (c % 2)] if 0 <= d < 32
]
UP = [(device(r, c), device(r - 1, c)) for r in range(1, 16) for c in range(32)]
DOWN = [(device(r, c), device(r + 1, c)) for r in range(15) for c in range(32)]


def body(matrix, moves):
    odd = lax.axis_index("col") % 2
    upper = lax.dynamic_slice(matrix, (odd * SPAN, BLOCK), (BLOCK, BLOCK))
    again = call(again_kernel, f32(BLOCK, BLOCK), [VMEM], VMEM, [], 0)(upper)
    join = call(join_kernel, f32(BLOCK, BLOCK), [VMEM] * 4, VMEM, [], 0)
    col_token = join(upper, *[send(upper, pairs) for pairs in ROWS_1])
    col_tokens = [col_token] + [send(col_token, pairs) for pairs in ROWS_2]
    row_token = join(again, *[send(again, pairs) for pairs in COLS_1])
    mine = call(sum_kernel, f32(BLOCK, BLOCK), [VMEM] * 4, VMEM, [], 0)(
        row_token, *[send(row_token, pairs) for pairs in COLS_2]
    )
    other = send(mine, CORES)

    half = f32(SPAN, BLOCK)
    held = [pltpu.VMEM((SPAN, SPAN), jnp.float32), pltpu.SemaphoreType.DMA(())]
    away, near, high, low = call(
        first_columns_kernel,
        (half, half, bf16(SPAN, SPAN), bf16(SPAN, SPAN)),
        [HBM] + [VMEM] * 4,
        (VMEM,) * 4,
        held,
        0,
    )(matrix, *col_tokens)
    parts = [(away, near, send(away, CHIPS), send(near, CORES))]
    away, near = call(more_columns_kernel, (half, half), [HBM, VMEM, VMEM], (VMEM,) * 2, held, 0)(matrix, high, low)
    parts.append((away, near, send(away, CHIPS), send(near, CORES)))

    high, low = call(rotations_kernel, (bf16(2, SPAN, SPAN),) * 2, [VMEM] * 2, (VMEM,) * 2, [], 0)(mine, other)
    wide = f32(BLOCK, SPAN)
    turn = [
        call(
            functools.partial(rows_kernel, pair),
            (wide, wide),
            [SMEM] + [VMEM] * 6,
            (VMEM,) * 2,
            [pltpu.VMEM((SPAN, SPAN), jnp.float32)],
            0,
        )
        for pair in range(2)
    ]
    first, second = turn[0](moves, *parts[0], high, low)
    below = send(first, UP)
    third, fourth = turn[1](moves, *parts[1], high, low)
    above = send(fourth, DOWN)
    partial = call(
        own_kernel, f32(*matrix.shape), [SMEM] + [VMEM] * 4, HBM, [pltpu.SemaphoreType.DMA((4,))], 0
    )(moves, first, second, third, fourth)
    return call(
        arrivals_kernel,
        f32(*matrix.shape),
        [SMEM] + [VMEM] * 2 + [HBM],
        HBM,
        [pltpu.SemaphoreType.DMA((2,))],
        0,
        aliases={3: 0},
    )(moves, above, below, partial)


def solution(mesh):
    placed = (P("row", "col"), P())
    return jax.shard_map(body, mesh=mesh, in_specs=placed, out_specs=P("row", "col"), check_vma=False)
```
